512 devices in a mesh: band: 32 (over y, x_lo, core), tile: 16 (over x_hi, z).
Axes of the slice: x: 4 (x_hi: 2, x_lo: 2; x = x_hi * 2 + x_lo), y: 8, z: 8, core: 2. Of those that a mesh axis runs over, the one named last changes fastest.
Arguments:
- frames: bfloat16 [16384, 128], P('tile'), may hold values from -6 to 6
- projection: bfloat16 [8192, 128], replicated, may hold values from -0.0625 to 0.0625
- offsets: int32 [32, 8], P('band'), may hold values from 0 to 16383
Outputs:
- profile: float32 [32, 16384], P('band', 'tile')
The draws below stay inside these ranges and needn't reach their ends.
All inputs are finite; a program needn't handle non-finite values.
Results may differ from the reference program's by a relative error of at most 0.0013.
Values may be sent and summed in bfloat16 or wider, within the bound.
A program may use at most 64 MiB of HBM per device.

```python
import math
import jax
import jax.numpy as jnp
from jax import lax

MEL = 128
SK = 128
WIN = 64
ROWS_DEV = 1024
NOFF = 8
S = 16384
N_BAND = 32


def place_ends(drawn, rng, low, high):
    index_at = [jax.random.randint(jax.random.fold_in(rng, axis), (), 0, length) for axis, length in enumerate(drawn.shape)]
    longest = drawn.shape.index(max(drawn.shape))
    beside = index_at[:longest] + [(index_at[longest] + 1) % drawn.shape[longest]] + index_at[longest + 1:]
    return drawn.at[tuple(index_at)].set(low).at[tuple(beside)].set(high)


def block_scale(key, dims, split, low, top_value):
    factor_of = 1.0
    for axis_at, shards_of in split:
        steps = jax.random.uniform(jax.random.fold_in(jax.random.fold_in(key, 6), axis_at), (shards_of,), jnp.float32, low / len(split), top_value / len(split))
        factor_of = factor_of * jnp.repeat(jnp.exp(steps), dims[axis_at] // shards_of).reshape((-1,) + (1,) * (len(dims) - 1 - axis_at))
    return factor_of


def gaussian(stream_key, shape, deviation, bound, shards=(), kind=jnp.bfloat16):
    entries = jax.random.normal(stream_key, shape, jnp.float32) * deviation
    if len(shards) > 0:
        entries = block_scale(stream_key, shape, shards, -0.22, 0.18) * entries
    return jnp.clip(entries, min=-bound, max=bound).astype(kind)


def setup_inputs(seed: int = 0) -> dict:
    key_list = jax.random.split(jax.random.key(seed), 4)
    frames = gaussian(key_list[0], (S, MEL), 1.0, 6.0, ((0, 16),))
    projection = gaussian(key_list[1], (WIN * MEL, SK), (WIN * MEL) ** -0.5, 0.0625)
    offsets = place_ends(jax.random.randint(key_list[2], (N_BAND, NOFF), 0, S), jax.random.fold_in(key_list[2], 1), 0, S - 1).astype(jnp.int32)
    return dict(frames=frames, projection=projection, offsets=offsets)


def make_sketch(extended, projection, count):
    width = math.gcd(count, 128)
    blocks = count // width
    channels = extended.shape[1]
    span = projection.shape[0] // channels

    def one_block(block):
        piece = lax.dynamic_slice_in_dim(extended, block * width, width + span - 1, 0)
        stacked = jnp.stack([piece[shift_k:shift_k + width] for shift_k in range(span)], axis=1)
        stacked = stacked.reshape(width, span * channels)
        return jnp.dot(stacked, projection, preferred_element_type=jnp.float32)
    values = lax.map(one_block, jnp.arange(blocks, dtype=jnp.int32))
    values = values.reshape(count, projection.shape[1])
    centred = values - lax.optimization_barrier(jnp.mean(values, axis=1, keepdims=True))
    scaled = centred * lax.rsqrt(lax.optimization_barrier(jnp.mean(centred * centred, axis=1, keepdims=True)) + 1e-05)
    return scaled.astype(jnp.bfloat16)

def reference(frames, projection, offsets):
    total = frames.shape[0]
    rows = ROWS_DEV
    blocks = total // rows
    width_sk = projection.shape[1]
    extended = jnp.concatenate([frames, jnp.zeros((WIN - 1, frames.shape[1]), frames.dtype)], axis=0)
    sketches = make_sketch(extended, projection, total)
    padded = jnp.concatenate([sketches, jnp.zeros((total, width_sk), sketches.dtype)], axis=0)
    row_blocks = sketches.reshape(blocks, rows, width_sk).astype(jnp.float32)
    row_index = jnp.arange(total, dtype=jnp.int32).reshape(blocks, rows, 1)

    def step(best, offset):
        col_blocks = lax.dynamic_slice_in_dim(padded, offset, total, 0)
        col_blocks = col_blocks.reshape(blocks, rows, width_sk).astype(jnp.float32)
        corr = jnp.einsum('tik,tjk->tij', row_blocks, col_blocks) / width_sk
        col_index = row_index.reshape(blocks, 1, rows) + offset
        valid = (col_index < total) & (jnp.abs(row_index - col_index) >= WIN)
        masked = jnp.where(valid, corr, jnp.float32(-2.0))
        row_best = lax.optimization_barrier(jnp.max(masked, axis=2)).reshape(total)
        col_best = lax.optimization_barrier(jnp.max(masked, axis=1)).reshape(total)
        best = best.at[:total].max(row_best)
        window = lax.dynamic_slice_in_dim(best, offset, total, 0)
        best = lax.dynamic_update_slice_in_dim(best, jnp.maximum(window, col_best), offset, 0)
        return (best, None)

    def per_band(band_offsets):
        start_best = jnp.full((2 * total,), -2.0, jnp.float32)
        best, _ = lax.scan(step, start_best, band_offsets.astype(jnp.int32))
        return best[:total]
    return lax.map(per_band, offsets.astype(jnp.int32))
```

```python
import functools

import jax
import jax.numpy as jnp
from jax import lax
from jax.experimental import pallas as pl
from jax.experimental.pallas import tpu as pltpu
from jax.sharding import PartitionSpec as P

MESH = pl.DeviceIdType.MESH
ROWS = 1024
HALF = 512
CH = 128
TAIL = 64
GROUP = 16
PIECES = 4
PIECE = HALF // PIECES
BANDS = 32
TILES = 16
NOFF = 8
LOW = -256.0


def pad_shift(value, by):
    return pltpu.roll(value, value.shape[0] - by, 0)


def sketch_rows(frames, proj):
    count = HALF + GROUP
    left = jnp.concatenate([frames[GROUP * a : GROUP * a + count] for a in range(4)], axis=1)

    def weights(c):
        return jnp.concatenate(
            [proj[(GROUP * a + c) * CH : (GROUP * a + c + 1) * CH, :] for a in range(4)], axis=0
        )

    def by_eight(c):
        right = jnp.concatenate([weights(c), weights(c + 8)], axis=1)
        both = jnp.dot(left, right, preferred_element_type=jnp.float32)
        return both[: HALF + 8, :CH] + both[8:, CH:]

    def by_four(c):
        return by_eight(c) + pad_shift(by_eight(c + 4), 4)

    def by_two(c):
        return by_four(c) + pad_shift(by_four(c + 2), 2)

    values = (by_two(0) + pad_shift(by_two(1), 1))[:HALF]
    centred = values - jnp.mean(values, axis=1, keepdims=True)
    scaled = centred * lax.rsqrt(jnp.mean(centred * centred, axis=1, keepdims=True) + 1e-05)
    return scaled.astype(jnp.bfloat16)


def corr_piece(piece, base, colsk, rowsk, xbuf):
    cols = colsk[PIECE * piece : PIECE * (piece + 1), :]
    apart = lax.broadcasted_iota(jnp.int32, (PIECE, 256), 1) - lax.broadcasted_iota(jnp.int32, (PIECE, 256), 0)
    for part in range(ROWS // 256):
        corr = lax.dot_general(
            cols,
            rowsk[256 * part : 256 * (part + 1), :],
            (((1,), (1,)), ((), ())),
            preferred_element_type=jnp.float32,
        )
        far = jnp.abs(apart + (base + 256 * part - PIECE * piece)) >= TAIL
        corr = jnp.where(far, corr, LOW)
        for side in range(2):
            xbuf[pl.ds(PIECE * piece * 8 + 2 * part + side, PIECE, stride=8), :] = corr[:, CH * side : CH * (side + 1)]


def column_of(xbuf, c):
    return xbuf[pl.ds(pl.multiple_of(c * 8, 8), 8), :]


def prefix_piece(piece, carry, xbuf, table):
    def step(c, best):
        best = jnp.maximum(best, column_of(xbuf, c))
        table[c + 1] = best
        return best

    return lax.fori_loop(PIECE * piece, PIECE * (piece + 1), step, carry, unroll=16)


def suffix_all(xbuf, table):
    low = jnp.full((8, CH), LOW, jnp.float32)
    table[2 * HALF] = low

    def step(k, best):
        c = HALF - 1 - k
        best = jnp.maximum(best, column_of(xbuf, c))
        table[HALF + c] = best
        return best

    lax.fori_loop(0, HALF, step, low, unroll=16)


def band_best(bb, isx, ksm, table, whole, place):
    best = jnp.full((8, CH), LOW, jnp.float32)
    for n in range(NOFF):
        best = jnp.maximum(best, table[isx[bb, n]])
        second = jnp.right_shift(place + ksm[bb, n], 10) == 0
        best = jnp.maximum(best, jnp.where(second, whole, LOW))
    return best * (1.0 / CH)


def kernel(
    frames, proj_hbm, offs, out, ext, proj, rowsk, colsk, xbuf, table, oall, ibuf, kbuf, isx, ksm, sbuf, rbuf,
    local_sem, tail_sem, offs_sem, half_sem, piece_send, piece_recv, out_sem,
):
    b, t = lax.axis_index("band"), lax.axis_index("tile")
    core, xl, y = lax.rem(b, 2), lax.rem(lax.div(b, 2), 2), lax.div(b, 4)
    xh, z = lax.div(t, 8), lax.rem(t, 8)
    partner = b + 1 - 2 * core
    chunk_block = xl * 8 + y
    base = (t - chunk_block) * ROWS - core * HALF

    load_frames = pltpu.make_async_copy(frames, ext.at[pl.ds(0, ROWS)], local_sem.at[0])
    load_frames.start()
    load_proj = pltpu.make_async_copy(proj_hbm, proj, local_sem.at[1])
    load_proj.start()

    def turned(step):
        return lax.rem(b + step, BANDS)

    def source(piece):
        ys = lax.rem(2 * piece + 1 - z - y + 16, 8)
        return (ys * 4 + (1 - xh) * 2 + core, xl * 8 + y)

    def target(piece):
        zt = lax.rem(2 * piece + 1 - z - y + 16, 8)
        return (z * 4 + xh * 2 + core, (1 - xl) * 8 + zt)

    barrier = pltpu.get_barrier_semaphore()

    def greet(step, carry):
        pl.semaphore_signal(barrier, inc=1, device_id=(turned(step), t), device_id_type=MESH)
        return carry

    pl.semaphore_signal(barrier, inc=1, device_id=(b, lax.rem(t + 1, TILES)), device_id_type=MESH)
    for piece in range(PIECES):
        pl.semaphore_signal(barrier, inc=1, device_id=source(piece), device_id_type=MESH)
    lax.fori_loop(1, BANDS, greet, 0)

    oall[pl.ds(b, 1), :] = jnp.zeros((1, CH), jnp.int32)
    oall[pl.ds(b, 1), 0:NOFF] = offs[...]
    pl.semaphore_wait(barrier, BANDS + PIECES)

    tail = pltpu.make_async_remote_copy(
        src_ref=frames.at[pl.ds(0, TAIL)],
        dst_ref=ext.at[pl.ds(ROWS, TAIL)],
        send_sem=tail_sem.at[0],
        recv_sem=tail_sem.at[1],
        device_id=(b, lax.rem(t + TILES - 1, TILES)),
        device_id_type=MESH,
    )
    tail.start()

    def offs_copy(rows, to):
        return pltpu.make_async_remote_copy(
            src_ref=oall.at[rows],
            dst_ref=oall.at[rows],
            send_sem=offs_sem.at[0],
            recv_sem=offs_sem.at[1],
            device_id=(to, t),
            device_id_type=MESH,
        )

    def send_offs(step, carry):
        offs_copy(pl.ds(b, 1), turned(step)).start()
        return carry

    lax.fori_loop(1, BANDS, send_offs, 0)

    load_frames.wait()
    load_proj.wait()
    tail.wait()

    @pl.when(t == TILES - 1)
    def _():
        ext[pl.ds(ROWS, TAIL), :] = jnp.zeros((TAIL, CH), jnp.bfloat16)

    mine = pl.ds(pl.multiple_of(core * HALF, HALF), HALF)
    rowsk[mine, :] = sketch_rows(ext[pl.ds(pl.multiple_of(core * HALF, HALF), HALF + TAIL), :], proj)

    half = pltpu.make_async_remote_copy(
        src_ref=rowsk.at[mine],
        dst_ref=rowsk.at[mine],
        send_sem=half_sem.at[0],
        recv_sem=half_sem.at[1],
        device_id=(partner, t),
        device_id_type=MESH,
    )
    pieces = [
        pltpu.make_async_remote_copy(
            src_ref=rowsk.at[pl.ds(pl.multiple_of(core * HALF + PIECE * piece, PIECE), PIECE)],
            dst_ref=colsk.at[pl.ds(PIECE * piece, PIECE)],
            send_sem=piece_send.at[piece],
            recv_sem=piece_recv.at[piece],
            device_id=target(piece),
            device_id_type=MESH,
        )
        for piece in range(PIECES)
    ]
    for copy in pieces:
        copy.start()
    half.start()

    offs_copy(pl.ds(0, BANDS - 1), b).wait()
    offsets = oall[...]
    reach = offsets + (base + ROWS)
    ibuf[...] = jnp.clip(reach, 0, HALF) + jnp.clip(reach - ROWS, 0, HALF)
    kbuf[...] = (t - chunk_block) * ROWS - offsets
    load_i = pltpu.make_async_copy(ibuf, isx, local_sem.at[2])
    load_k = pltpu.make_async_copy(kbuf, ksm, local_sem.at[3])
    load_i.start()
    load_k.start()
    half.wait_recv()

    low = jnp.full((8, CH), LOW, jnp.float32)
    table[0] = low
    whole = low
    for piece in range(PIECES):
        pieces[piece].wait_recv()
        corr_piece(piece, base, colsk, rowsk, xbuf)
        whole = prefix_piece(piece, whole, xbuf, table)
    suffix_all(xbuf, table)
    load_i.wait()
    load_k.wait()

    place = lax.broadcasted_iota(jnp.int32, (8, CH), 0) * CH + lax.broadcasted_iota(jnp.int32, (8, CH), 1)

    def out_copy(src, dst, to):
        return pltpu.make_async_remote_copy(
            src_ref=sbuf.at[src],
            dst_ref=rbuf.at[dst],
            send_sem=out_sem.at[0],
            recv_sem=out_sem.at[1],
            device_id=(to, t),
            device_id_type=MESH,
        )

    def send_best(step, carry):
        bb = turned(step)
        sbuf[bb] = band_best(bb, isx, ksm, table, whole, place)
        out_copy(pl.ds(bb, 1), pl.ds(b, 1), bb).start()
        return carry

    lax.fori_loop(1, BANDS, send_best, 0)
    rbuf[b] = band_best(b, isx, ksm, table, whole, place)

    every = out_copy(pl.ds(0, BANDS - 1), pl.ds(0, BANDS - 1), b)
    every.wait_recv()
    out[...] = jnp.max(rbuf[...], axis=0)
    every.wait_send()
    half.wait_send()
    for copy in pieces:
        copy.wait_send()


def shards(frames, projection, offsets):
    dma = pltpu.SemaphoreType.DMA
    best = pl.pallas_call(
        kernel,
        out_shape=jax.ShapeDtypeStruct((8, CH), jnp.float32),
        in_specs=[
            pl.BlockSpec(memory_space=pl.ANY),
            pl.BlockSpec(memory_space=pl.ANY),
            pl.BlockSpec(memory_space=pltpu.VMEM),
        ],
        out_specs=pl.BlockSpec(memory_space=pltpu.VMEM),
        scratch_shapes=[
            pltpu.VMEM((ROWS + TAIL, CH), jnp.bfloat16),
            pltpu.VMEM((TAIL * CH, CH), jnp.bfloat16),
            pltpu.VMEM((ROWS, CH), jnp.bfloat16),
            pltpu.VMEM((HALF, CH), jnp.bfloat16),
            pltpu.VMEM((HALF * 8, CH), jnp.float32),
            pltpu.VMEM((2 * HALF + 1, 8, CH), jnp.float32),
            pltpu.VMEM((BANDS, CH), jnp.int32),
            pltpu.VMEM((BANDS, CH), jnp.int32),
            pltpu.VMEM((BANDS, CH), jnp.int32),
            pltpu.SMEM((BANDS, CH), jnp.int32),
            pltpu.SMEM((BANDS, CH), jnp.int32),
            pltpu.VMEM((BANDS, 8, CH), jnp.float32),
            pltpu.VMEM((BANDS, 8, CH), jnp.float32),
            dma((4,)),
            dma((2,)),
            dma((2,)),
            dma((2,)),
            dma((PIECES,)),
            dma((PIECES,)),
            dma((2,)),
        ],
        compiler_params=pltpu.CompilerParams(
            collective_id=0, has_side_effects=True, vmem_limit_bytes=48 * 1024 * 1024
        ),
    )(frames, projection, offsets)
    return best.reshape(1, ROWS)


def solution(mesh):
    in_specs = (P("tile", None), P(), P("band", None))
    out_specs = P("band", "tile")
    return jax.shard_map(shards, mesh=mesh, in_specs=in_specs, out_specs=out_specs, check_vma=False)
```

```python
import functools

import jax
import jax.numpy as jnp
from jax import lax
from jax.experimental import pallas as pl
from jax.experimental.pallas import tpu as pltpu
from jax.sharding import PartitionSpec as P

MESH = pl.DeviceIdType.MESH
ROWS = 1024
HALF = 512
CH = 128
TAIL = 64
GROUP = 16
PIECES = 4
PIECE = HALF // PIECES
BANDS = 32
CHIPS = 16
TILES = 16
NOFF = 8
LOW = -256.0


def pad_shift(value, by):
    return pltpu.roll(value, value.shape[0] - by, 0)


def sketch_rows(frames, proj):
    count = HALF + GROUP
    left = jnp.concatenate([frames[GROUP * a : GROUP * a + count] for a in range(4)], axis=1)

    def weights(c):
        return jnp.concatenate(
            [proj[(GROUP * a + c) * CH : (GROUP * a + c + 1) * CH, :] for a in range(4)], axis=0
        )

    def by_eight(c):
        right = jnp.concatenate([weights(c), weights(c + 8)], axis=1)
        both = jnp.dot(left, right, preferred_element_type=jnp.float32)
        return both[: HALF + 8, :CH] + both[8:, CH:]

    def by_four(c):
        return by_eight(c) + pad_shift(by_eight(c + 4), 4)

    def by_two(c):
        return by_four(c) + pad_shift(by_four(c + 2), 2)

    values = (by_two(0) + pad_shift(by_two(1), 1))[:HALF]
    centred = values - jnp.mean(values, axis=1, keepdims=True)
    scaled = centred * lax.rsqrt(jnp.mean(centred * centred, axis=1, keepdims=True) + 1e-05)
    return scaled.astype(jnp.bfloat16)


def corr_piece(piece, base, colsk, rowsk, xbuf):
    cols = colsk[PIECE * piece : PIECE * (piece + 1), :]
    apart = lax.broadcasted_iota(jnp.int32, (PIECE, 256), 1) - lax.broadcasted_iota(jnp.int32, (PIECE, 256), 0)
    for part in range(ROWS // 256):
        corr = lax.dot_general(
            cols,
            rowsk[256 * part : 256 * (part + 1), :],
            (((1,), (1,)), ((), ())),
            preferred_element_type=jnp.float32,
        )
        far = jnp.abs(apart + (base + 256 * part - PIECE * piece)) >= TAIL
        corr = jnp.where(far, corr, LOW)
        for side in range(2):
            xbuf[pl.ds(PIECE * piece * 8 + 2 * part + side, PIECE, stride=8), :] = corr[:, CH * side : CH * (side + 1)]


def column_of(xbuf, c):
    return xbuf[pl.ds(pl.multiple_of(c * 8, 8), 8), :]


def prefix_piece(piece, carry, xbuf, table):
    def step(c, best):
        best = jnp.maximum(best, column_of(xbuf, c))
        table[c + 1] = best
        return best

    return lax.fori_loop(PIECE * piece, PIECE * (piece + 1), step, carry, unroll=16)


def suffix_all(xbuf, table):
    low = jnp.full((8, CH), LOW, jnp.float32)
    table[2 * HALF] = low

    def step(k, best):
        c = HALF - 1 - k
        best = jnp.maximum(best, column_of(xbuf, c))
        table[HALF + c] = best
        return best

    lax.fori_loop(0, HALF, step, low, unroll=16)


def band_best(band, isx, ksm, table, whole, place):
    best = jnp.full((8, CH), LOW, jnp.float32)
    for n in range(NOFF):
        best = jnp.maximum(best, table[isx[band, n]])
        second = jnp.right_shift(place + ksm[band, n], 10) == 0
        best = jnp.maximum(best, jnp.where(second, whole, LOW))
    return best * (1.0 / CH)


def kernel(
    frames, proj_hbm, offs, out, ext, cext, proj, rowsk, colsk, xbuf, table, oall, ibuf, kbuf, isx, ksm, sbuf, rbuf,
    fin, other, local_sem, tail_sem, cols_send, cols_recv, offs_send, offs_recv, out_sem, fin_sem,
):
    b, t = lax.axis_index("band"), lax.axis_index("tile")
    core, xl, y = lax.rem(b, 2), lax.rem(lax.div(b, 2), 2), lax.div(b, 4)
    xh, z = lax.div(t, 8), lax.rem(t, 8)
    chip = lax.div(b, 2)
    zs = jnp.where(y < 4, 7 - 2 * y, 2 * y - 8)
    chunk_block = xl * 8 + zs
    base = (t - chunk_block) * ROWS - core * HALF
    partner = (b + 1 - 2 * core, t)
    beside = (b + 2 - 4 * xl, t)
    up = (lax.rem(b + 4, BANDS), t)
    down = (lax.rem(b + BANDS - 4, BANDS), t)
    is_source = z == zs
    on_diagonal = xl == xh
    is_own = jnp.logical_and(is_source, on_diagonal)
    swapped = y * 4 + xh * 2 + core

    def remote(src, dst, send_sem, recv_sem, to):
        return pltpu.make_async_remote_copy(
            src_ref=src, dst_ref=dst, send_sem=send_sem, recv_sem=recv_sem, device_id=to, device_id_type=MESH
        )

    load_frames = pltpu.make_async_copy(frames, ext.at[pl.ds(0, ROWS)], local_sem.at[0])
    load_frames.start()
    load_proj = pltpu.make_async_copy(proj_hbm, proj, local_sem.at[1])
    load_proj.start()

    barrier = pltpu.get_barrier_semaphore()

    @pl.when(jnp.logical_not(is_own))
    def _():
        pl.semaphore_signal(barrier, inc=1, device_id=(swapped, chunk_block), device_id_type=MESH)

    for peer in ((b, lax.rem(t + 1, TILES)), up, down, beside, partner):
        pl.semaphore_signal(barrier, inc=1, device_id=peer, device_id_type=MESH)

    oall[pl.ds(b, 1), :] = jnp.zeros((1, CH), jnp.int32)
    oall[pl.ds(b, 1), 0:NOFF] = offs[...]
    targets = jnp.where(is_source, jnp.where(on_diagonal, 7, 8), 0)
    pl.semaphore_wait(barrier, 5 + targets)

    tail = remote(
        frames.at[pl.ds(0, TAIL)], ext.at[pl.ds(ROWS, TAIL)], tail_sem.at[0], tail_sem.at[1],
        (b, lax.rem(t + TILES - 1, TILES)),
    )
    tail.start()

    def offs_copy(rows, at, to):
        return remote(oall.at[rows], oall.at[rows], offs_send.at[at], offs_recv.at[at], to)

    def row_of(behind):
        return pl.ds(lax.rem(y + behind + 8, 8) * 4, 4)

    to_partner = offs_copy(pl.ds(b, 1), 0, partner)
    to_beside = offs_copy(pl.ds(chip * 2, 2), 1, beside)
    rise = [offs_copy(row_of(-k), 2 + k, up) for k in range(4)]
    fall = [offs_copy(row_of(k), 6 + k, down) for k in range(3)]
    to_partner.start()

    load_frames.wait()
    tail.wait_recv()

    @pl.when(t == TILES - 1)
    def _():
        ext[pl.ds(ROWS, TAIL), :] = jnp.zeros((TAIL, CH), jnp.bfloat16)

    part = pl.ds(pl.multiple_of(core * HALF, HALF), HALF + TAIL)

    def cols_copy(zt):
        return remote(ext.at[part], cext, cols_send.at[zt], cols_recv.at[0], (swapped, xl * 8 + zt))

    cols_own = pltpu.make_async_copy(ext.at[part], cext, cols_recv.at[0])
    for zt in range(8):
        own = jnp.logical_and(is_own, z == zt)

        @pl.when(jnp.logical_and(is_source, jnp.logical_not(own)))
        def _():
            cols_copy(zt).start()

        @pl.when(own)
        def _():
            cols_own.start()

    to_partner.wait_recv()
    to_beside.start()
    load_proj.wait()
    rowsk[0:HALF, :] = sketch_rows(ext[0 : HALF + TAIL, :], proj)
    to_beside.wait_recv()
    rise[0].start()
    fall[0].start()
    rowsk[HALF:ROWS, :] = sketch_rows(ext[HALF : ROWS + TAIL, :], proj)
    for k in range(4):
        rise[k].wait_recv()
        if k < 3:
            rise[k + 1].start()
            fall[k].wait_recv()
        if k < 2:
            fall[k + 1].start()

    offsets = oall[...]
    reach = offsets + (base + ROWS)
    ibuf[...] = jnp.clip(reach, 0, HALF) + jnp.clip(reach - ROWS, 0, HALF)
    kbuf[...] = (t - chunk_block) * ROWS - offsets
    load_i = pltpu.make_async_copy(ibuf, isx, local_sem.at[2])
    load_k = pltpu.make_async_copy(kbuf, ksm, local_sem.at[3])
    load_i.start()
    load_k.start()

    cols_own.wait()
    colsk[...] = sketch_rows(cext[...], proj)

    low = jnp.full((8, CH), LOW, jnp.float32)
    table[0] = low
    whole = low
    for piece in range(PIECES):
        corr_piece(piece, base, colsk, rowsk, xbuf)
        whole = prefix_piece(piece, whole, xbuf, table)
    suffix_all(xbuf, table)
    load_i.wait()
    load_k.wait()

    place = lax.broadcasted_iota(jnp.int32, (8, CH), 0) * CH + lax.broadcasted_iota(jnp.int32, (8, CH), 1)

    def out_copy(src, dst, to):
        return remote(sbuf.at[src], rbuf.at[dst], out_sem.at[0], out_sem.at[1], (to * 2 + core, t))

    def send_best(k, carry):
        step = 8 + jnp.where(lax.rem(k, 2) == 1, lax.div(k + 1, 2), -lax.div(k, 2))
        to = lax.rem(chip + step, CHIPS)
        for side in range(2):
            sbuf[to, side] = band_best(to * 2 + side, isx, ksm, table, whole, place)
        out_copy(pl.ds(to, 1), pl.ds(chip, 1), to).start()
        return carry

    lax.fori_loop(0, CHIPS - 1, send_best, 0)
    for side in range(2):
        rbuf[chip, side] = band_best(chip * 2 + side, isx, ksm, table, whole, place)

    every = out_copy(pl.ds(0, CHIPS - 1), pl.ds(0, CHIPS - 1), chip)
    every.wait_recv()
    fin[...] = jnp.max(rbuf[...], axis=0)
    swap = remote(fin.at[pl.ds(1 - core, 1)], other, fin_sem.at[0], fin_sem.at[1], partner)
    swap.start()
    swap.wait_recv()
    best = jnp.maximum(fin[core], other[0])
    for group in range(8):
        out[:, CH * group : CH * (group + 1)] = best[group : group + 1, :]

    swap.wait_send()
    every.wait_send()
    tail.wait_send()
    to_partner.wait_send()
    to_beside.wait_send()
    for copy in rise + fall:
        copy.wait_send()
    for zt in range(8):

        @pl.when(jnp.logical_and(is_source, jnp.logical_not(jnp.logical_and(is_own, z == zt))))
        def _():
            cols_copy(zt).wait_send()


def shards(frames, projection, offsets):
    dma = pltpu.SemaphoreType.DMA
    return pl.pallas_call(
        kernel,
        out_shape=jax.ShapeDtypeStruct((1, ROWS), jnp.float32),
        in_specs=[
            pl.BlockSpec(memory_space=pl.ANY),
            pl.BlockSpec(memory_space=pl.ANY),
            pl.BlockSpec(memory_space=pltpu.VMEM),
        ],
        out_specs=pl.BlockSpec(memory_space=pltpu.VMEM),
        scratch_shapes=[
            pltpu.VMEM((ROWS + TAIL, CH), jnp.bfloat16),
            pltpu.VMEM((HALF + TAIL, CH), jnp.bfloat16),
            pltpu.VMEM((TAIL * CH, CH), jnp.bfloat16),
            pltpu.VMEM((ROWS, CH), jnp.bfloat16),
            pltpu.VMEM((HALF, CH), jnp.bfloat16),
            pltpu.VMEM((HALF * 8, CH), jnp.float32),
            pltpu.VMEM((2 * HALF + 1, 8, CH), jnp.float32),
            pltpu.VMEM((BANDS, CH), jnp.int32),
            pltpu.VMEM((BANDS, CH), jnp.int32),
            pltpu.VMEM((BANDS, CH), jnp.int32),
            pltpu.SMEM((BANDS, CH), jnp.int32),
            pltpu.SMEM((BANDS, CH), jnp.int32),
            pltpu.VMEM((CHIPS, 2, 8, CH), jnp.float32),
            pltpu.VMEM((CHIPS, 2, 8, CH), jnp.float32),
            pltpu.VMEM((2, 8, CH), jnp.float32),
            pltpu.VMEM((1, 8, CH), jnp.float32),
            dma((4,)),
            dma((2,)),
            dma((8,)),
            dma((1,)),
            dma((9,)),
            dma((9,)),
            dma((2,)),
            dma((2,)),
        ],
        compiler_params=pltpu.CompilerParams(
            collective_id=0, has_side_effects=True, vmem_limit_bytes=62 * 1024 * 1024
        ),
    )(frames, projection, offsets)


def solution(mesh):
    in_specs = (P("tile", None), P(), P("band", None))
    out_specs = P("band", "tile")
    return jax.shard_map(shards, mesh=mesh, in_specs=in_specs, out_specs=out_specs, check_vma=False)
```

```python
import functools

import jax
import jax.numpy as jnp
from jax import lax
from jax.experimental import pallas as pl
from jax.experimental.pallas import tpu as pltpu
from jax.sharding import PartitionSpec as P

MESH = pl.DeviceIdType.MESH
ROWS = 1024
HALF = 512
CH = 128
TAIL = 64
GROUP = 16
PIECES = 4
PIECE = HALF // PIECES
BANDS = 32
CHIPS = 16
TILES = 16
NOFF = 8
LOW = -256.0


def pad_shift(value, by):
    return pltpu.roll(value, value.shape[0] - by, 0)


def sketch_rows(frames, proj):
    count = HALF + GROUP
    left = jnp.concatenate([frames[GROUP * a : GROUP * a + count] for a in range(4)], axis=1)

    def weights(c):
        return jnp.concatenate(
            [proj[(GROUP * a + c) * CH : (GROUP * a + c + 1) * CH, :] for a in range(4)], axis=0
        )

    def by_eight(c):
        right = jnp.concatenate([weights(c), weights(c + 8)], axis=1)
        both = jnp.dot(left, right, preferred_element_type=jnp.float32)
        return both[: HALF + 8, :CH] + both[8:, CH:]

    def by_four(c):
        return by_eight(c) + pad_shift(by_eight(c + 4), 4)

    def by_two(c):
        return by_four(c) + pad_shift(by_four(c + 2), 2)

    values = (by_two(0) + pad_shift(by_two(1), 1))[:HALF]
    centred = values - jnp.mean(values, axis=1, keepdims=True)
    scaled = centred * lax.rsqrt(jnp.mean(centred * centred, axis=1, keepdims=True) + 1e-05)
    return scaled.astype(jnp.bfloat16)


def corr_piece(piece, base, colsk, rowsk, xbuf):
    cols = colsk[PIECE * piece : PIECE * (piece + 1), :]
    apart = lax.broadcasted_iota(jnp.int32, (PIECE, 256), 1) - lax.broadcasted_iota(jnp.int32, (PIECE, 256), 0)
    for part in range(ROWS // 256):
        corr = lax.dot_general(
            cols,
            rowsk[256 * part : 256 * (part + 1), :],
            (((1,), (1,)), ((), ())),
            preferred_element_type=jnp.float32,
        )
        far = jnp.abs(apart + (base + 256 * part - PIECE * piece)) >= TAIL
        corr = jnp.where(far, corr, LOW)
        for side in range(2):
            xbuf[pl.ds(PIECE * piece * 8 + 2 * part + side, PIECE, stride=8), :] = corr[:, CH * side : CH * (side + 1)]


def column_of(xbuf, c):
    return xbuf[pl.ds(pl.multiple_of(c * 8, 8), 8), :]


def running_best(xbuf, table):
    low = jnp.full((8, CH), LOW, jnp.float32)
    table[0] = low
    table[2 * HALF] = low

    def step(c, carry):
        first, last = carry
        first = jnp.maximum(first, column_of(xbuf, c))
        table[c + 1] = first
        d = HALF - 1 - c
        last = jnp.maximum(last, column_of(xbuf, d))
        table[HALF + d] = last

        return first, last

    return lax.fori_loop(0, HALF, step, (low, low), unroll=16)[0]


def band_best(band, isx, ksm, table, whole, place):
    best = jnp.full((8, CH), LOW, jnp.float32)
    for n in range(NOFF):
        best = jnp.maximum(best, table[isx[band, n]])
        second = jnp.right_shift(place + ksm[band, n], 10) == 0
        best = jnp.maximum(best, jnp.where(second, whole, LOW))
    return best * (1.0 / CH)


def kernel(
    frames, proj_hbm, offs_hbm, out, offs, ext, cext, proj, rowsk, colsk, xbuf, table, oall, ibuf, kbuf, isx, ksm, sbuf, rbuf,
    fin, other, local_sem, tail_sem, pass_send, cols_send, next_send, cols_recv, offs_send, offs_recv, out_sem, fin_sem,
):
    b, t = lax.axis_index("band"), lax.axis_index("tile")
    core, xl, y = lax.rem(b, 2), lax.rem(lax.div(b, 2), 2), lax.div(b, 4)
    xh, z = lax.div(t, 8), lax.rem(t, 8)
    chip = lax.div(b, 2)
    zs = lax.rem(jnp.where(y < 4, 2 * y, 15 - 2 * y) + 4 * core, 8)
    chunk_block = xl * 8 + zs
    base = (t - chunk_block) * ROWS - core * HALF
    partner = (b + 1 - 2 * core, t)
    after, before = lax.rem(t + 1, TILES), lax.rem(t + TILES - 1, TILES)
    is_source = z == zs
    is_next = jnp.logical_and(lax.rem(before, 8) == zs, core == 1)
    source_own = jnp.logical_and(is_source, xl == xh)
    next_own = jnp.logical_and(t == lax.rem(chunk_block + 1, TILES), jnp.logical_and(xl == xh, core == 1))
    next_on_line = lax.div(before, 8) == xl
    swapped = y * 4 + xh * 2 + core
    gets_tail = jnp.logical_or(z != 7, y == 0)
    gives_tail = jnp.logical_or(z != 0, y == 0)

    def remote(src, dst, send_sem, recv_sem, to):
        return pltpu.make_async_remote_copy(
            src_ref=src, dst_ref=dst, send_sem=send_sem, recv_sem=recv_sem, device_id=to, device_id_type=MESH
        )

    load_frames = pltpu.make_async_copy(frames, ext.at[pl.ds(0, ROWS)], local_sem.at[0])
    load_offs = pltpu.make_async_copy(offs_hbm, offs, local_sem.at[4])
    load_offs.start()
    load_frames.start()
    load_proj = pltpu.make_async_copy(proj_hbm, proj, local_sem.at[1])
    load_proj.start()

    barrier = pltpu.get_barrier_semaphore()

    def greet(to):
        pl.semaphore_signal(barrier, inc=1, device_id=to, device_id_type=MESH)

    def along(step):
        return (lax.rem(chip + step, CHIPS) * 2 + core, t)

    @pl.when(jnp.logical_not(source_own))
    def _():
        greet((swapped, chunk_block))

    @pl.when(jnp.logical_and(core == 1, jnp.logical_not(next_own)))
    def _():
        greet((swapped, lax.rem(chunk_block + 1, TILES)))

    @pl.when(gets_tail)
    def _():
        greet((b, after))

    greet(partner)

    def greet_chip(step, carry):
        greet(along(step))
        return carry

    lax.fori_loop(1, CHIPS, greet_chip, 0)

    oall[pl.ds(b, 1), :] = jnp.zeros((1, CH), jnp.int32)
    load_offs.wait()
    oall[pl.ds(b, 1), 0:NOFF] = offs[...]
    as_source = jnp.where(is_source, jnp.where(xl == xh, 7, 8), 0)
    as_next = jnp.where(is_next, jnp.where(jnp.logical_and(next_on_line, xl == xh), 7, 8), 0)
    pl.semaphore_wait(barrier, CHIPS + as_source + as_next + jnp.where(gives_tail, 1, 0))

    tail_at = ext.at[pl.ds(ROWS, TAIL)]
    tail = remote(frames.at[pl.ds(0, TAIL)], tail_at, tail_sem.at[0], tail_sem.at[1], (b, before))

    @pl.when(gives_tail)
    def _():
        tail.start()

    def cols_copy(zt, rows):
        part = pl.ds(pl.multiple_of(core * HALF, HALF), rows)
        return remote(
            frames.at[part], cext.at[pl.ds(0, rows)], cols_send.at[zt], cols_recv.at[0], (swapped, xl * 8 + zt)
        )

    def cols_own(rows):
        part = pl.ds(pl.multiple_of(core * HALF, HALF), rows)
        return pltpu.make_async_copy(frames.at[part], cext.at[pl.ds(0, rows)], cols_recv.at[0])

    def next_copy(zt):
        to = (y * 4 + lax.div(before, 8) * 2 + core, xl * 8 + zt)
        return remote(frames.at[pl.ds(0, TAIL)], cext.at[pl.ds(HALF, TAIL)], next_send.at[zt], cols_recv.at[1], to)

    next_copy_own = pltpu.make_async_copy(frames.at[pl.ds(0, TAIL)], cext.at[pl.ds(HALF, TAIL)], cols_recv.at[1])

    def sized(what):
        @pl.when(core == 0)
        def _():
            what(HALF + TAIL)

        @pl.when(core == 1)
        def _():
            what(HALF)

    def each_target(cols_do, next_do, cols_do_own, next_do_own):
        @pl.when(is_source)
        def _():
            for zt in range(8):
                own = jnp.logical_and(source_own, z == zt)

                @pl.when(jnp.logical_not(own))
                def _():
                    sized(functools.partial(cols_do, zt))

                if cols_do_own is not None:

                    @pl.when(own)
                    def _():
                        sized(cols_do_own)

        @pl.when(is_next)
        def _():
            for zt in range(8):
                own = jnp.logical_and(next_own, z == zt)

                @pl.when(jnp.logical_not(own))
                def _():
                    next_do(zt)

                if next_do_own is not None:

                    @pl.when(own)
                    def _():
                        next_do_own()

    each_target(
        lambda zt, rows: cols_copy(zt, rows).start(),
        lambda zt: next_copy(zt).start(),
        lambda rows: cols_own(rows).start(),
        lambda: next_copy_own.start(),
    )

    def offs_copy(rows, at, to):
        return remote(oall.at[rows], oall.at[rows], offs_send.at[at], offs_recv.at[at], to)

    to_partner = offs_copy(pl.ds(b, 1), 0, partner)
    to_partner.start()
    to_partner.wait_recv()

    def send_offs(step, carry):
        offs_copy(pl.ds(chip * 2, 2), 1, along(step)).start()
        return carry

    lax.fori_loop(1, CHIPS, send_offs, 0)

    load_frames.wait()
    load_proj.wait()
    rowsk[0:HALF, :] = sketch_rows(ext[0 : HALF + TAIL, :], proj)
    tail.wait_recv()

    @pl.when(t == TILES - 1)
    def _():
        ext[pl.ds(ROWS, TAIL), :] = jnp.zeros((TAIL, CH), jnp.bfloat16)

    passes_on = jnp.logical_and(z == 7, y == 0)

    def pass_on(yt):
        return remote(tail_at, tail_at, pass_send.at[yt], tail_sem.at[1], (b + 4 * yt, t))

    @pl.when(passes_on)
    def _():
        for yt in range(1, 8):
            pass_on(yt).start()

    rowsk[HALF:ROWS, :] = sketch_rows(ext[HALF : ROWS + TAIL, :], proj)
    every_offs = offs_copy(pl.ds(0, BANDS - 2), 1, along(1))
    every_offs.wait_recv()

    offsets = oall[...]
    reach = offsets + (base + ROWS)
    ibuf[...] = jnp.clip(reach, 0, HALF) + jnp.clip(reach - ROWS, 0, HALF)
    kbuf[...] = (t - chunk_block) * ROWS - offsets
    load_i = pltpu.make_async_copy(ibuf, isx, local_sem.at[2])
    load_k = pltpu.make_async_copy(kbuf, ksm, local_sem.at[3])
    load_i.start()
    load_k.start()

    sized(lambda rows: cols_own(rows).wait())

    @pl.when(core == 1)
    def _():
        next_copy_own.wait()

    @pl.when(jnp.logical_and(core == 1, chunk_block == TILES - 1))
    def _():
        cext[pl.ds(HALF, TAIL), :] = jnp.zeros((TAIL, CH), jnp.bfloat16)

    colsk[...] = sketch_rows(cext[...], proj)

    for piece in range(PIECES):
        corr_piece(piece, base, colsk, rowsk, xbuf)
    whole = running_best(xbuf, table)
    load_i.wait()
    load_k.wait()

    place = lax.broadcasted_iota(jnp.int32, (8, CH), 0) * CH + lax.broadcasted_iota(jnp.int32, (8, CH), 1)

    def out_copy(src, dst, to):
        return remote(sbuf.at[src], rbuf.at[dst], out_sem.at[0], out_sem.at[1], (to * 2 + core, t))

    def send_best(k, carry):
        step = 8 + jnp.where(lax.rem(k, 2) == 1, lax.div(k + 1, 2), -lax.div(k, 2))
        to = lax.rem(chip + step, CHIPS)
        for side in range(2):
            sbuf[to, side] = band_best(to * 2 + side, isx, ksm, table, whole, place)
        out_copy(pl.ds(to, 1), pl.ds(chip, 1), to).start()
        return carry

    lax.fori_loop(0, CHIPS - 1, send_best, 0)
    for side in range(2):
        rbuf[chip, side] = band_best(chip * 2 + side, isx, ksm, table, whole, place)

    every = out_copy(pl.ds(0, CHIPS - 1), pl.ds(0, CHIPS - 1), chip)
    every.wait_recv()
    fin[...] = jnp.max(rbuf[...], axis=0)
    swap = remote(fin.at[pl.ds(1 - core, 1)], other, fin_sem.at[0], fin_sem.at[1], partner)
    swap.start()
    swap.wait_recv()
    best = jnp.maximum(fin[core], other[0])
    for group in range(8):
        out[:, CH * group : CH * (group + 1)] = best[group : group + 1, :]

    swap.wait_send()
    every.wait_send()
    to_partner.wait_send()
    every_offs.wait_send()

    @pl.when(gives_tail)
    def _():
        tail.wait_send()

    @pl.when(passes_on)
    def _():
        for yt in range(1, 8):
            pass_on(yt).wait_send()

    each_target(
        lambda zt, rows: cols_copy(zt, rows).wait_send(), lambda zt: next_copy(zt).wait_send(), None, None
    )


def shards(frames, projection, offsets):
    dma = pltpu.SemaphoreType.DMA
    return pl.pallas_call(
        kernel,
        out_shape=jax.ShapeDtypeStruct((1, ROWS), jnp.float32),
        in_specs=[
            pl.BlockSpec(memory_space=pl.ANY),
            pl.BlockSpec(memory_space=pl.ANY),
            pl.BlockSpec(memory_space=pl.ANY),
        ],
        out_specs=pl.BlockSpec(memory_space=pltpu.VMEM),
        scratch_shapes=[
            pltpu.VMEM((1, NOFF), jnp.int32),
            pltpu.VMEM((ROWS + TAIL, CH), jnp.bfloat16),
            pltpu.VMEM((HALF + TAIL, CH), jnp.bfloat16),
            pltpu.VMEM((TAIL * CH, CH), jnp.bfloat16),
            pltpu.VMEM((ROWS, CH), jnp.bfloat16),
            pltpu.VMEM((HALF, CH), jnp.bfloat16),
            pltpu.VMEM((HALF * 8, CH), jnp.float32),
            pltpu.VMEM((2 * HALF + 1, 8, CH), jnp.float32),
            pltpu.VMEM((BANDS, CH), jnp.int32),
            pltpu.VMEM((BANDS, CH), jnp.int32),
            pltpu.VMEM((BANDS, CH), jnp.int32),
            pltpu.SMEM((BANDS, CH), jnp.int32),
            pltpu.SMEM((BANDS, CH), jnp.int32),
            pltpu.VMEM((CHIPS, 2, 8, CH), jnp.float32),
            pltpu.VMEM((CHIPS, 2, 8, CH), jnp.float32),
            pltpu.VMEM((2, 8, CH), jnp.float32),
            pltpu.VMEM((1, 8, CH), jnp.float32),
            dma((5,)),
            dma((2,)),
            dma((8,)),
            dma((8,)),
            dma((8,)),
            dma((2,)),
            dma((2,)),
            dma((2,)),
            dma((2,)),
            dma((2,)),
        ],
        compiler_params=pltpu.CompilerParams(
            collective_id=0, has_side_effects=True, vmem_limit_bytes=62 * 1024 * 1024
        ),
    )(frames, projection, offsets)


def solution(mesh):
    in_specs = (P("tile", None), P(), P("band", None))
    out_specs = P("band", "tile")
    return jax.shard_map(shards, mesh=mesh, in_specs=in_specs, out_specs=out_specs, check_vma=False)
```

```python
import functools

import jax
import jax.numpy as jnp
from jax import lax
from jax.experimental import pallas as pl
from jax.experimental.pallas import tpu as pltpu
from jax.sharding import PartitionSpec as P

MESH = pl.DeviceIdType.MESH
ROWS = 1024
HALF = 512
CH = 128
TAIL = 64
GROUP = 16
PIECES = 4
PIECE = HALF // PIECES
BANDS = 32
CHIPS = 16
TILES = 16
NOFF = 8
LOW = -256.0
STEPS = 254
NONE = -32768


def pad_shift(value, by):
    return pltpu.roll(value, value.shape[0] - by, 0)


def sketch_rows(frames, proj):
    count = HALF + GROUP
    left = jnp.concatenate([frames[GROUP * a : GROUP * a + count] for a in range(4)], axis=1)

    def weights(c):
        return jnp.concatenate(
            [proj[(GROUP * a + c) * CH : (GROUP * a + c + 1) * CH, :] for a in range(4)], axis=0
        )

    def by_eight(c):
        right = jnp.concatenate([weights(c), weights(c + 8)], axis=1)
        both = jnp.dot(left, right, preferred_element_type=jnp.float32)
        return both[: HALF + 8, :CH] + both[8:, CH:]

    def by_four(c):
        return by_eight(c) + pad_shift(by_eight(c + 4), 4)

    def by_two(c):
        return by_four(c) + pad_shift(by_four(c + 2), 2)

    values = (by_two(0) + pad_shift(by_two(1), 1))[:HALF]
    centred = values - jnp.mean(values, axis=1, keepdims=True)
    scaled = centred * lax.rsqrt(jnp.mean(centred * centred, axis=1, keepdims=True) + 1e-05)
    return scaled.astype(jnp.bfloat16)


def corr_piece(piece, base, colsk, rowsk, xbuf):
    cols = colsk[PIECE * piece : PIECE * (piece + 1), :]
    apart = lax.broadcasted_iota(jnp.int32, (PIECE, 256), 1) - lax.broadcasted_iota(jnp.int32, (PIECE, 256), 0)
    for part in range(ROWS // 256):
        corr = lax.dot_general(
            cols,
            rowsk[256 * part : 256 * (part + 1), :],
            (((1,), (1,)), ((), ())),
            preferred_element_type=jnp.float32,
        )
        far = jnp.abs(apart + (base + 256 * part - PIECE * piece)) >= TAIL
        corr = jnp.where(far, corr, LOW)
        for side in range(2):
            xbuf[pl.ds(PIECE * piece * 8 + 2 * part + side, PIECE, stride=8), :] = corr[:, CH * side : CH * (side + 1)]


def column_of(xbuf, c):
    return xbuf[pl.ds(pl.multiple_of(c * 8, 8), 8), :]


def running_best(xbuf, table):
    low = jnp.full((8, CH), LOW, jnp.float32)
    table[0] = low
    table[2 * HALF] = low

    def step(c, carry):
        first, last = carry
        first = jnp.maximum(first, column_of(xbuf, c))
        table[c + 1] = first
        d = HALF - 1 - c
        last = jnp.maximum(last, column_of(xbuf, d))
        table[HALF + d] = last

        return first, last

    return lax.fori_loop(0, HALF, step, (low, low), unroll=16)[0]


def band_best(band, isx, ksm, table, whole, place):
    best = jnp.full((8, CH), LOW, jnp.float32)
    for n in range(NOFF):
        best = jnp.maximum(best, table[isx[band, n]])
        second = jnp.right_shift(place + ksm[band, n], 10) == 0
        best = jnp.maximum(best, jnp.where(second, whole, LOW))
    return best


def joined_z(y, core):
    pair = lax.div(y, 2)
    low = jnp.where(pair == 0, 0, jnp.where(pair == 1, 3, pair - 1))
    return low + 4 * lax.rem(y + core, 2)


def sends_blocks(y, z, core):
    closes = jnp.logical_and(core == 0, lax.rem(joined_z(y, 1) + 1, 8) == z)
    return jnp.logical_or(joined_z(y, core) == z, closes)


def kernel(
    frames, proj_hbm, offs_hbm, out, offs, ext, cext, proj, rowsk, colsk, xbuf, table, oall, ibuf, kbuf, isx, ksm, sbuf, rbuf,
    fin, other, local_sem, tail_sem, pass_send, cols_send, next_send, cols_recv, offs_send, offs_recv, out_sem, fin_sem, ready,
):
    b, t = lax.axis_index("band"), lax.axis_index("tile")
    core, xl, y = lax.rem(b, 2), lax.rem(lax.div(b, 2), 2), lax.div(b, 4)
    xh, z = lax.div(t, 8), lax.rem(t, 8)
    chip = lax.div(b, 2)
    zs = joined_z(y, core)
    chunk_block = xl * 8 + zs
    base = (t - chunk_block) * ROWS - core * HALF
    partner = (b + 1 - 2 * core, t)
    after, before = lax.rem(t + 1, TILES), lax.rem(t + TILES - 1, TILES)
    early = z < 4
    is_source = z == zs
    source_own = jnp.logical_and(is_source, xl == xh)
    is_next = jnp.logical_and(lax.rem(before, 8) == joined_z(y, 1), core == 0)
    next_xh = lax.div(before, 8)
    sends = sends_blocks(y, z, core)
    other_sends = sends_blocks(y, z, 1 - core)
    gets_tail = jnp.logical_or(z != 7, y == 0)
    gives_tail = jnp.logical_or(z != 0, y == 0)

    def remote(src, dst, send_sem, recv_sem, to):
        return pltpu.make_async_remote_copy(
            src_ref=src, dst_ref=dst, send_sem=send_sem, recv_sem=recv_sem, device_id=to, device_id_type=MESH
        )

    load_frames = pltpu.make_async_copy(frames, ext.at[pl.ds(0, ROWS)], local_sem.at[0])
    load_offs = pltpu.make_async_copy(offs_hbm, offs, local_sem.at[4])
    load_offs.start()
    load_frames.start()
    load_proj = pltpu.make_async_copy(proj_hbm, proj, local_sem.at[1])
    load_proj.start()

    barrier = pltpu.get_barrier_semaphore()

    def greet(to):
        pl.semaphore_signal(barrier, inc=1, device_id=to, device_id_type=MESH)

    def along(step):
        return (lax.rem(chip + step, CHIPS) * 2 + core, t)

    @pl.when(jnp.logical_not(source_own))
    def _():
        greet((y * 4 + xh * 2 + jnp.where(early, core, 1 - core), chunk_block))

    @pl.when(core == 1)
    def _():
        greet((y * 4 + xh * 2 + jnp.where(early, 0, 1), lax.rem(chunk_block + 1, TILES)))

    @pl.when(gets_tail)
    def _():
        greet((b, after))

    greet(partner)

    def greet_chip(step, carry):
        to = lax.rem(chip + step, CHIPS)
        swapped = sends_blocks(lax.div(to, 2), z, core)
        greet((to * 2 + jnp.where(swapped, 1 - core, core), t))
        return carry

    lax.fori_loop(1, CHIPS, greet_chip, 0)

    oall[pl.ds(b, 1), :] = jnp.zeros((1, CH), jnp.int32)
    load_offs.wait()
    oall[pl.ds(b, 1), 0:NOFF] = offs[...]
    def targets(is_one, own, own_here):
        return jnp.where(is_one, 4 - jnp.where(jnp.logical_and(own, own_here), 1, 0), 0)

    other_source = z == joined_z(y, 1 - core)
    other_next = jnp.logical_and(lax.rem(before, 8) == joined_z(y, 1), core == 1)
    as_source = targets(is_source, xl == xh, early) + jnp.where(is_next, 4, 0)
    as_next = targets(other_source, xl == xh, jnp.logical_not(early)) + jnp.where(other_next, 4, 0)
    as_band = jnp.where(sends, 0, CHIPS - 1) + jnp.where(other_sends, CHIPS - 1, 0)
    pl.semaphore_wait(barrier, 1 + as_source + as_next + as_band + jnp.where(gives_tail, 1, 0))

    tail_at = ext.at[pl.ds(ROWS, TAIL)]
    tail = remote(frames.at[pl.ds(0, TAIL)], tail_at, tail_sem.at[0], tail_sem.at[1], (b, before))

    @pl.when(gives_tail)
    def _():
        tail.start()

    def cols_copy(zt, rows):
        part = pl.ds(pl.multiple_of(core * HALF, HALF), rows)
        to = (y * 4 + xh * 2 + core, xl * 8 + zt)
        return remote(frames.at[part], cext.at[pl.ds(0, rows)], cols_send.at[zt], cols_recv.at[0], to)

    def cols_own(rows):
        part = pl.ds(pl.multiple_of(core * HALF, HALF), rows)
        return pltpu.make_async_copy(frames.at[part], cext.at[pl.ds(0, rows)], cols_recv.at[0])

    close_at = cext.at[pl.ds(HALF, TAIL)]

    def next_copy(zt):
        to = (y * 4 + next_xh * 2 + 1, xl * 8 + zt)
        return remote(frames.at[pl.ds(0, TAIL)], close_at, next_send.at[zt], cols_recv.at[1], to)

    def sized(what):
        @pl.when(core == 0)
        def _():
            what(HALF + TAIL)

        @pl.when(core == 1)
        def _():
            what(HALF)

    def each_target(zts, cols_do, next_do, cols_do_own):
        @pl.when(is_next)
        def _():
            for zt in zts:
                next_do(zt)

        @pl.when(is_source)
        def _():
            for zt in zts:
                own = jnp.logical_and(source_own, z == zt)

                @pl.when(jnp.logical_not(own))
                def _():
                    sized(functools.partial(cols_do, zt))

                if cols_do_own is not None:

                    @pl.when(own)
                    def _():
                        sized(cols_do_own)

    def start_to(zts):
        each_target(
            zts,
            lambda zt, rows: cols_copy(zt, rows).start(),
            lambda zt: next_copy(zt).start(),
            lambda rows: cols_own(rows).start(),
        )

    start_to(range(4))

    @pl.when(other_sends)
    def _():
        pl.semaphore_signal(ready, inc=1, device_id=partner, device_id_type=MESH)

    @pl.when(sends)
    def _():
        pl.semaphore_wait(ready, 1)

    start_to(range(4, 8))

    def offs_copy(rows, at, to):
        return remote(oall.at[rows], oall.at[rows], offs_send.at[at], offs_recv.at[at], to)

    to_partner = offs_copy(pl.ds(b, 1), 0, partner)
    to_partner.start()
    to_partner.wait_recv()

    def send_offs(step, carry):
        offs_copy(pl.ds(chip * 2, 2), 1, along(step)).start()
        return carry

    lax.fori_loop(1, CHIPS, send_offs, 0)

    load_frames.wait()
    load_proj.wait()
    rowsk[0:HALF, :] = sketch_rows(ext[0 : HALF + TAIL, :], proj)
    tail.wait_recv()

    @pl.when(t == TILES - 1)
    def _():
        ext[pl.ds(ROWS, TAIL), :] = jnp.zeros((TAIL, CH), jnp.bfloat16)

    passes_on = jnp.logical_and(z == 7, y == 0)

    def pass_on(yt):
        return remote(tail_at, tail_at, pass_send.at[yt], tail_sem.at[1], (b + 4 * yt, t))

    @pl.when(passes_on)
    def _():
        for yt in range(1, 8):
            pass_on(yt).start()

    rowsk[HALF:ROWS, :] = sketch_rows(ext[HALF : ROWS + TAIL, :], proj)
    sized(lambda rows: cols_own(rows).wait())

    @pl.when(core == 1)
    def _():
        pltpu.make_async_copy(frames.at[pl.ds(0, TAIL)], close_at, cols_recv.at[1]).wait()

    @pl.when(jnp.logical_and(core == 1, chunk_block == TILES - 1))
    def _():
        cext[pl.ds(HALF, TAIL), :] = jnp.zeros((TAIL, CH), jnp.bfloat16)

    colsk[...] = sketch_rows(cext[...], proj)

    for piece in range(PIECES):
        corr_piece(piece, base, colsk, rowsk, xbuf)
    every_offs = offs_copy(pl.ds(0, BANDS - 2), 1, along(1))
    every_offs.wait_recv()

    offsets = oall[...]
    reach = offsets + (base + ROWS)
    ibuf[...] = jnp.clip(reach, 0, HALF) + jnp.clip(reach - ROWS, 0, HALF)
    kbuf[...] = (t - chunk_block) * ROWS - offsets
    load_i = pltpu.make_async_copy(ibuf, isx, local_sem.at[2])
    load_k = pltpu.make_async_copy(kbuf, ksm, local_sem.at[3])
    load_i.start()
    load_k.start()

    whole = running_best(xbuf, table)
    load_i.wait()
    load_k.wait()

    place = lax.broadcasted_iota(jnp.int32, (8, CH), 0) * CH + lax.broadcasted_iota(jnp.int32, (8, CH), 1)

    def out_copy(src, dst, to):
        return remote(sbuf.at[src], rbuf.at[dst], out_sem.at[0], out_sem.at[1], (to * 2 + core, t))

    def coded(to):
        both = [band_best(to * 2 + side, isx, ksm, table, whole, place) for side in range(2)]
        scaled = jnp.maximum(jnp.concatenate(both, axis=0) * STEPS, NONE)
        return jnp.round(scaled).astype(jnp.int32).astype(jnp.int16)

    def send_best(k, carry):
        step = 8 + jnp.where(lax.rem(k, 2) == 1, lax.div(k + 1, 2), -lax.div(k, 2))
        to = lax.rem(chip + step, CHIPS)
        sbuf[to] = coded(to)
        out_copy(pl.ds(to, 1), pl.ds(chip, 1), to).start()
        return carry

    lax.fori_loop(0, CHIPS - 1, send_best, 0)
    rbuf[chip] = coded(chip)

    every = out_copy(pl.ds(0, CHIPS - 1), pl.ds(0, CHIPS - 1), chip)
    every.wait_recv()
    top = rbuf[0].astype(jnp.int32)
    for k in range(1, CHIPS):
        top = jnp.maximum(top, rbuf[k].astype(jnp.int32))
    fin[0] = top[0:8]
    fin[1] = top[8:16]
    swap = remote(fin.at[pl.ds(1 - core, 1)], other, fin_sem.at[0], fin_sem.at[1], partner)
    swap.start()
    swap.wait_recv()
    code = jnp.maximum(fin[core], other[0])
    best = jnp.where(code == NONE, -2.0, code.astype(jnp.float32) * (1.0 / (STEPS * CH)))
    for group in range(8):
        out[:, CH * group : CH * (group + 1)] = best[group : group + 1, :]

    swap.wait_send()
    every.wait_send()
    to_partner.wait_send()
    every_offs.wait_send()

    @pl.when(gives_tail)
    def _():
        tail.wait_send()

    @pl.when(passes_on)
    def _():
        for yt in range(1, 8):
            pass_on(yt).wait_send()

    each_target(range(8), lambda zt, rows: cols_copy(zt, rows).wait_send(), lambda zt: next_copy(zt).wait_send(), None)


def shards(frames, projection, offsets):
    dma = pltpu.SemaphoreType.DMA
    return pl.pallas_call(
        kernel,
        out_shape=jax.ShapeDtypeStruct((1, ROWS), jnp.float32),
        in_specs=[
            pl.BlockSpec(memory_space=pl.ANY),
            pl.BlockSpec(memory_space=pl.ANY),
            pl.BlockSpec(memory_space=pl.ANY),
        ],
        out_specs=pl.BlockSpec(memory_space=pltpu.VMEM),
        scratch_shapes=[
            pltpu.VMEM((1, NOFF), jnp.int32),
            pltpu.VMEM((ROWS + TAIL, CH), jnp.bfloat16),
            pltpu.VMEM((HALF + TAIL, CH), jnp.bfloat16),
            pltpu.VMEM((TAIL * CH, CH), jnp.bfloat16),
            pltpu.VMEM((ROWS, CH), jnp.bfloat16),
            pltpu.VMEM((HALF, CH), jnp.bfloat16),
            pltpu.VMEM((HALF * 8, CH), jnp.float32),
            pltpu.VMEM((2 * HALF + 1, 8, CH), jnp.float32),
            pltpu.VMEM((BANDS, CH), jnp.int32),
            pltpu.VMEM((BANDS, CH), jnp.int32),
            pltpu.VMEM((BANDS, CH), jnp.int32),
            pltpu.SMEM((BANDS, CH), jnp.int32),
            pltpu.SMEM((BANDS, CH), jnp.int32),
            pltpu.VMEM((CHIPS, 16, CH), jnp.int16),
            pltpu.VMEM((CHIPS, 16, CH), jnp.int16),
            pltpu.VMEM((2, 8, CH), jnp.int32),
            pltpu.VMEM((1, 8, CH), jnp.int32),
            dma((5,)),
            dma((2,)),
            dma((8,)),
            dma((8,)),
            dma((8,)),
            dma((2,)),
            dma((2,)),
            dma((2,)),
            dma((2,)),
            dma((2,)),
            pltpu.SemaphoreType.REGULAR,
        ],
        compiler_params=pltpu.CompilerParams(
            collective_id=0, has_side_effects=True, vmem_limit_bytes=62 * 1024 * 1024
        ),
    )(frames, projection, offsets)


def solution(mesh):
    in_specs = (P("tile", None), P(), P("band", None))
    out_specs = P("band", "tile")
    return jax.shard_map(shards, mesh=mesh, in_specs=in_specs, out_specs=out_specs, check_vma=False)
```

```python
import functools

import jax
import jax.numpy as jnp
from jax import lax
from jax.experimental import pallas as pl
from jax.experimental.pallas import tpu as pltpu
from jax.sharding import PartitionSpec as P

MESH = pl.DeviceIdType.MESH
ROWS = 1024
HALF = 512
CH = 128
TAIL = 64
GROUP = 16
PIECES = 4
PIECE = HALF // PIECES
BANDS = 32
CHIPS = 16
TILES = 16
NOFF = 8
GRANT = (54 * 1024 - 128) * 1024
LOW = -256.0
STEPS = 254
NONE = -32768


def pad_shift(value, by):
    return pltpu.roll(value, value.shape[0] - by, 0)


def sketch_rows(frames, proj):
    count = HALF + GROUP
    left = jnp.concatenate([frames[GROUP * a : GROUP * a + count] for a in range(4)], axis=1)

    def weights(c):
        return jnp.concatenate(
            [proj[(GROUP * a + c) * CH : (GROUP * a + c + 1) * CH, :] for a in range(4)], axis=0
        )

    def by_eight(c):
        right = jnp.concatenate([weights(c), weights(c + 8)], axis=1)
        both = jnp.dot(left, right, preferred_element_type=jnp.float32)
        return both[: HALF + 8, :CH] + both[8:, CH:]

    def by_four(c):
        return by_eight(c) + pad_shift(by_eight(c + 4), 4)

    def by_two(c):
        return by_four(c) + pad_shift(by_four(c + 2), 2)

    values = (by_two(0) + pad_shift(by_two(1), 1))[:HALF]
    centred = values - jnp.mean(values, axis=1, keepdims=True)
    scaled = centred * lax.rsqrt(jnp.mean(centred * centred, axis=1, keepdims=True) + 1e-05)
    return scaled.astype(jnp.bfloat16)


def corr_piece(piece, base, colsk, rowsk, xbuf):
    cols = colsk[PIECE * piece : PIECE * (piece + 1), :]
    apart = lax.broadcasted_iota(jnp.int32, (PIECE, 256), 1) - lax.broadcasted_iota(jnp.int32, (PIECE, 256), 0)
    for part in range(ROWS // 256):
        corr = lax.dot_general(
            cols,
            rowsk[256 * part : 256 * (part + 1), :],
            (((1,), (1,)), ((), ())),
            preferred_element_type=jnp.float32,
        )
        far = jnp.abs(apart + (base + 256 * part - PIECE * piece)) >= TAIL
        corr = jnp.where(far, corr, LOW)
        for side in range(2):
            xbuf[pl.ds(PIECE * piece * 8 + 2 * part + side, PIECE, stride=8), :] = corr[:, CH * side : CH * (side + 1)]


def column_of(xbuf, c):
    return xbuf[pl.ds(pl.multiple_of(c * 8, 8), 8), :]


def running_best(xbuf, table):
    low = jnp.full((8, CH), LOW, jnp.float32)
    table[0] = low
    table[2 * HALF] = low

    def step(c, carry):
        first, last = carry
        first = jnp.maximum(first, column_of(xbuf, c))
        table[c + 1] = first
        d = HALF - 1 - c
        last = jnp.maximum(last, column_of(xbuf, d))
        table[HALF + d] = last

        return first, last

    return lax.fori_loop(0, HALF, step, (low, low), unroll=16)[0]


def band_best(band, isx, ksm, table, whole, place):
    best = jnp.full((8, CH), LOW, jnp.float32)
    for n in range(NOFF):
        best = jnp.maximum(best, table[isx[band, n]])
        second = jnp.right_shift(place + ksm[band, n], 10) == 0
        best = jnp.maximum(best, jnp.where(second, whole, LOW))
    return best


def joined_z(y, core):
    pair = lax.div(y, 2)
    low = jnp.where(pair == 0, 0, jnp.where(pair == 1, 3, pair - 1))
    return low + 4 * lax.rem(y + core, 2)


def sends_blocks(y, z, core):
    closes = jnp.logical_and(core == 0, lax.rem(joined_z(y, 1) + 1, 8) == z)
    return jnp.logical_or(joined_z(y, core) == z, closes)


def kernel(
    frames, proj_hbm, offs, out, ext, cext, proj, rowsk, colsk, xbuf, table, oall, ibuf, kbuf, isx, ksm, sbuf, rbuf,
    fin, other, local_sem, tail_sem, pass_send, cols_send, next_send, cols_recv, offs_send, offs_recv, out_sem, fin_sem, ready,
):
    b, t = lax.axis_index("band"), lax.axis_index("tile")
    core, xl, y = lax.rem(b, 2), lax.rem(lax.div(b, 2), 2), lax.div(b, 4)
    xh, z = lax.div(t, 8), lax.rem(t, 8)
    chip = lax.div(b, 2)
    zs = joined_z(y, core)
    chunk_block = xl * 8 + zs
    base = (t - chunk_block) * ROWS - core * HALF
    partner = (b + 1 - 2 * core, t)
    after, before = lax.rem(t + 1, TILES), lax.rem(t + TILES - 1, TILES)
    early = z < 4
    is_source = z == zs
    source_own = jnp.logical_and(is_source, xl == xh)
    is_next = jnp.logical_and(lax.rem(before, 8) == joined_z(y, 1), core == 0)
    next_xh = lax.div(before, 8)
    sends = sends_blocks(y, z, core)
    other_sends = sends_blocks(y, z, 1 - core)
    gets_tail = jnp.logical_or(z != 7, y == 0)
    gives_tail = jnp.logical_or(z != 0, y == 0)

    def remote(src, dst, send_sem, recv_sem, to):
        return pltpu.make_async_remote_copy(
            src_ref=src, dst_ref=dst, send_sem=send_sem, recv_sem=recv_sem, device_id=to, device_id_type=MESH
        )

    load_frames = pltpu.make_async_copy(frames, ext.at[pl.ds(0, ROWS)], local_sem.at[0])
    load_frames.start()
    load_proj = pltpu.make_async_copy(proj_hbm, proj, local_sem.at[1])
    load_proj.start()

    barrier = pltpu.get_barrier_semaphore()

    def greet(to):
        pl.semaphore_signal(barrier, inc=1, device_id=to, device_id_type=MESH)

    def along(step):
        return (lax.rem(chip + step, CHIPS) * 2 + core, t)

    @pl.when(jnp.logical_not(source_own))
    def _():
        greet((y * 4 + xh * 2 + jnp.where(early, core, 1 - core), chunk_block))

    @pl.when(core == 1)
    def _():
        greet((y * 4 + xh * 2 + jnp.where(early, 0, 1), lax.rem(chunk_block + 1, TILES)))

    @pl.when(gets_tail)
    def _():
        greet((b, after))

    greet(partner)

    def greet_chip(step, carry):
        to = lax.rem(chip + step, CHIPS)
        swapped = sends_blocks(lax.div(to, 2), z, core)
        greet((to * 2 + jnp.where(swapped, 1 - core, core), t))
        return carry

    lax.fori_loop(1, CHIPS, greet_chip, 0)

    oall[pl.ds(b, 1), :] = jnp.zeros((1, CH), jnp.int32)
    oall[pl.ds(b, 1), 0:NOFF] = offs[...]
    def targets(is_one, own, own_here):
        return jnp.where(is_one, 4 - jnp.where(jnp.logical_and(own, own_here), 1, 0), 0)

    other_source = z == joined_z(y, 1 - core)
    other_next = jnp.logical_and(lax.rem(before, 8) == joined_z(y, 1), core == 1)
    as_source = targets(is_source, xl == xh, early) + jnp.where(is_next, 4, 0)
    as_next = targets(other_source, xl == xh, jnp.logical_not(early)) + jnp.where(other_next, 4, 0)
    as_band = jnp.where(sends, 0, CHIPS - 1) + jnp.where(other_sends, CHIPS - 1, 0)
    pl.semaphore_wait(barrier, 1 + as_source + as_next + as_band + jnp.where(gives_tail, 1, 0))

    tail_at = ext.at[pl.ds(ROWS, TAIL)]
    tail = remote(frames.at[pl.ds(0, TAIL)], tail_at, tail_sem.at[0], tail_sem.at[1], (b, before))

    @pl.when(gives_tail)
    def _():
        tail.start()

    def cols_copy(zt, rows):
        part = pl.ds(pl.multiple_of(core * HALF, HALF), rows)
        to = (y * 4 + xh * 2 + core, xl * 8 + zt)
        return remote(frames.at[part], cext.at[pl.ds(0, rows)], cols_send.at[zt], cols_recv.at[0], to)

    def cols_own(rows):
        part = pl.ds(pl.multiple_of(core * HALF, HALF), rows)
        return pltpu.make_async_copy(frames.at[part], cext.at[pl.ds(0, rows)], cols_recv.at[0])

    close_at = cext.at[pl.ds(HALF, TAIL)]

    def next_copy(zt):
        to = (y * 4 + next_xh * 2 + 1, xl * 8 + zt)
        return remote(frames.at[pl.ds(0, TAIL)], close_at, next_send.at[zt], cols_recv.at[1], to)

    def sized(what):
        @pl.when(core == 0)
        def _():
            what(HALF + TAIL)

        @pl.when(core == 1)
        def _():
            what(HALF)

    def each_target(zts, cols_do, next_do, cols_do_own):
        @pl.when(is_next)
        def _():
            for zt in zts:
                next_do(zt)

        @pl.when(is_source)
        def _():
            for zt in zts:
                own = jnp.logical_and(source_own, z == zt)

                @pl.when(jnp.logical_not(own))
                def _():
                    sized(functools.partial(cols_do, zt))

                if cols_do_own is not None:

                    @pl.when(own)
                    def _():
                        sized(cols_do_own)

    def start_to(zts):
        each_target(
            zts,
            lambda zt, rows: cols_copy(zt, rows).start(),
            lambda zt: next_copy(zt).start(),
            lambda rows: cols_own(rows).start(),
        )

    start_to(range(4))

    @pl.when(other_sends)
    def _():
        pl.semaphore_signal(ready, inc=1, device_id=partner, device_id_type=MESH)

    @pl.when(sends)
    def _():
        pl.semaphore_wait(ready, 1)

    start_to(range(4, 8))

    def offs_copy(rows, at, to):
        return remote(oall.at[rows], oall.at[rows], offs_send.at[at], offs_recv.at[at], to)

    to_partner = offs_copy(pl.ds(b, 1), 0, partner)
    to_partner.start()
    to_partner.wait_recv()

    def send_offs(step, carry):
        offs_copy(pl.ds(chip * 2, 2), 1, along(step)).start()
        return carry

    lax.fori_loop(1, CHIPS, send_offs, 0)

    load_frames.wait()
    load_proj.wait()
    rowsk[0:HALF, :] = sketch_rows(ext[0 : HALF + TAIL, :], proj)
    tail.wait_recv()

    @pl.when(t == TILES - 1)
    def _():
        ext[pl.ds(ROWS, TAIL), :] = jnp.zeros((TAIL, CH), jnp.bfloat16)

    passes_on = jnp.logical_and(z == 7, y == 0)

    def pass_on(yt):
        return remote(tail_at, tail_at, pass_send.at[yt], tail_sem.at[1], (b + 4 * yt, t))

    @pl.when(passes_on)
    def _():
        for yt in range(1, 8):
            pass_on(yt).start()

    rowsk[HALF:ROWS, :] = sketch_rows(ext[HALF : ROWS + TAIL, :], proj)
    sized(lambda rows: cols_own(rows).wait())

    @pl.when(core == 1)
    def _():
        pltpu.make_async_copy(frames.at[pl.ds(0, TAIL)], close_at, cols_recv.at[1]).wait()

    @pl.when(jnp.logical_and(core == 1, chunk_block == TILES - 1))
    def _():
        cext[pl.ds(HALF, TAIL), :] = jnp.zeros((TAIL, CH), jnp.bfloat16)

    colsk[...] = sketch_rows(cext[...], proj)

    for piece in range(PIECES):
        corr_piece(piece, base, colsk, rowsk, xbuf)
    every_offs = offs_copy(pl.ds(0, BANDS - 2), 1, along(1))
    every_offs.wait_recv()

    offsets = oall[...]
    reach = offsets + (base + ROWS)
    ibuf[...] = jnp.clip(reach, 0, HALF) + jnp.clip(reach - ROWS, 0, HALF)
    kbuf[...] = (t - chunk_block) * ROWS - offsets
    load_i = pltpu.make_async_copy(ibuf, isx, local_sem.at[2])
    load_k = pltpu.make_async_copy(kbuf, ksm, local_sem.at[3])
    load_i.start()
    load_k.start()

    whole = running_best(xbuf, table)
    load_i.wait()
    load_k.wait()

    place = lax.broadcasted_iota(jnp.int32, (8, CH), 0) * CH + lax.broadcasted_iota(jnp.int32, (8, CH), 1)

    def out_copy(src, dst, to):
        return remote(sbuf.at[src], rbuf.at[dst], out_sem.at[0], out_sem.at[1], (to * 2 + core, t))

    def coded(to):
        both = [band_best(to * 2 + side, isx, ksm, table, whole, place) for side in range(2)]
        scaled = jnp.maximum(jnp.concatenate(both, axis=0) * STEPS, NONE)
        return jnp.round(scaled).astype(jnp.int32).astype(jnp.int16)

    def send_best(k, carry):
        step = 8 + jnp.where(lax.rem(k, 2) == 1, lax.div(k + 1, 2), -lax.div(k, 2))
        to = lax.rem(chip + step, CHIPS)
        sbuf[to] = coded(to)
        out_copy(pl.ds(to, 1), pl.ds(chip, 1), to).start()
        return carry

    lax.fori_loop(0, CHIPS - 1, send_best, 0)
    rbuf[chip] = coded(chip)

    every = out_copy(pl.ds(0, CHIPS - 1), pl.ds(0, CHIPS - 1), chip)
    every.wait_recv()
    top = rbuf[0].astype(jnp.int32)
    for k in range(1, CHIPS):
        top = jnp.maximum(top, rbuf[k].astype(jnp.int32))
    fin[0] = top[0:8]
    fin[1] = top[8:16]
    swap = remote(fin.at[pl.ds(1 - core, 1)], other, fin_sem.at[0], fin_sem.at[1], partner)
    swap.start()
    swap.wait_recv()
    code = jnp.maximum(fin[core], other[0])
    best = jnp.where(code == NONE, -2.0, code.astype(jnp.float32) * (1.0 / (STEPS * CH)))
    for group in range(8):
        out[:, CH * group : CH * (group + 1)] = best[group : group + 1, :]

    swap.wait_send()
    every.wait_send()
    to_partner.wait_send()
    every_offs.wait_send()

    @pl.when(gives_tail)
    def _():
        tail.wait_send()

    @pl.when(passes_on)
    def _():
        for yt in range(1, 8):
            pass_on(yt).wait_send()

    each_target(range(8), lambda zt, rows: cols_copy(zt, rows).wait_send(), lambda zt: next_copy(zt).wait_send(), None)


def shards(frames, projection, offsets):
    dma = pltpu.SemaphoreType.DMA
    return pl.pallas_call(
        kernel,
        out_shape=jax.ShapeDtypeStruct((1, ROWS), jnp.float32),
        in_specs=[
            pl.BlockSpec(memory_space=pl.ANY),
            pl.BlockSpec(memory_space=pl.ANY),
            pl.BlockSpec(memory_space=pltpu.VMEM),
        ],
        out_specs=pl.BlockSpec(memory_space=pltpu.VMEM),
        scratch_shapes=[
            pltpu.VMEM((ROWS + TAIL, CH), jnp.bfloat16),
            pltpu.VMEM((HALF + TAIL, CH), jnp.bfloat16),
            pltpu.VMEM((TAIL * CH, CH), jnp.bfloat16),
            pltpu.VMEM((ROWS, CH), jnp.bfloat16),
            pltpu.VMEM((HALF, CH), jnp.bfloat16),
            pltpu.VMEM((HALF * 8, CH), jnp.float32),
            pltpu.VMEM((2 * HALF + 1, 8, CH), jnp.float32),
            pltpu.VMEM((BANDS, CH), jnp.int32),
            pltpu.VMEM((BANDS, CH), jnp.int32),
            pltpu.VMEM((BANDS, CH), jnp.int32),
            pltpu.SMEM((BANDS, CH), jnp.int32),
            pltpu.SMEM((BANDS, CH), jnp.int32),
            pltpu.VMEM((CHIPS, 16, CH), jnp.int16),
            pltpu.VMEM((CHIPS, 16, CH), jnp.int16),
            pltpu.VMEM((2, 8, CH), jnp.int32),
            pltpu.VMEM((1, 8, CH), jnp.int32),
            dma((4,)),
            dma((2,)),
            dma((8,)),
            dma((8,)),
            dma((8,)),
            dma((2,)),
            dma((2,)),
            dma((2,)),
            dma((2,)),
            dma((2,)),
            pltpu.SemaphoreType.REGULAR,
        ],
        compiler_params=pltpu.CompilerParams(
            collective_id=0, has_side_effects=True, vmem_limit_bytes=GRANT
        ),
    )(frames, projection, offsets)


def solution(mesh):
    in_specs = (P("tile", None), P(), P("band", None))
    out_specs = P("band", "tile")
    return jax.shard_map(shards, mesh=mesh, in_specs=in_specs, out_specs=out_specs, check_vma=False)
```
